256 devices in a mesh: ctx: 16 (over z, core), ch: 16 (over x, y).
Axes of the slice: x: 4, y: 4, z: 8, core: 2. Of those that a mesh axis runs over, the one named last changes fastest.
Arguments:
- tokens: bfloat16 [24576, 4096], P('ctx', 'ch'), may hold values from -6 to 6
- in_weight: bfloat16 [4096, 3, 4096], P('ctx', None, 'ch'), may hold values from -0.09375 to 0.09375
- short_taps: float32 [3, 3, 4096], P(None, None, 'ch'), may hold values from -3 to 3
- residues: float32 [16, 4096], P(None, 'ch'), may hold values from -0.6 to 0.6
- decay_rates: float32 [16, 4096], P(None, 'ch'), may hold values from 2.0345053e-05 to 0.05
- skip_gain: float32 [4096], P('ch'), may hold values from -4 to 4
Outputs:
- mixed: bfloat16 [24576, 4096], P('ctx', 'ch')
The draws below stay inside these ranges and needn't reach their ends.
All inputs are finite; a program needn't handle non-finite values.
Results may differ from the reference program's by a relative error of at most 0.0065.
Values may be sent and summed in bfloat16 or wider, within the bound.
A program may use at most 128 MiB of HBM per device.

```python
import math
import jax
import jax.numpy as jnp
from jax import lax

D = 4096
POLES = 16
TAPS = 3
BLOCK = 32
TOKENS = 24576


def block_scale(key, shape, cuts, smallest, top_value):
    loudness = 1.0
    for dim, shards_of in cuts:
        draws = jax.random.uniform(jax.random.fold_in(jax.random.fold_in(key, 6), dim), (shards_of,), jnp.float32, smallest / len(cuts), top_value / len(cuts))
        loudness = loudness * jnp.repeat(jnp.exp(draws), shape[dim] // shards_of).reshape((-1,) + (1,) * (len(shape) - 1 - dim))
    return loudness


def normal_values(rng, dims, spread, reach, split=(), kind=jnp.bfloat16):
    loudness = block_scale(rng, dims, split, -0.22, 0.18) if split else 1.0
    drawn = jax.random.normal(rng, dims, jnp.float32) * spread * loudness
    return jnp.minimum(jnp.maximum(drawn, -reach), reach).astype(kind)


def setup_inputs(seed: int = 0) -> dict:
    streams_of = jax.random.split(jax.random.key(seed), 7)
    tokens = normal_values(streams_of[0], (TOKENS, D), 1.0, 6.0, ((0, 16), (1, 16)))
    in_weight = normal_values(streams_of[1], (D, 3, D), D ** -0.5, 0.09375, ((0, 16), (2, 16)))
    short_taps = normal_values(streams_of[2], (3, TAPS, D), 0.6, 3.0, ((2, 16),), jnp.float32)
    residues = normal_values(streams_of[3], (POLES, D), 0.1, 0.6, ((1, 16),), jnp.float32)
    decay_rates = jnp.clip(jnp.exp(math.log(0.05) - 7.8069405 * jax.random.uniform(streams_of[4], (POLES, D), jnp.float32) ** block_scale(streams_of[4], (POLES, D), ((1, 16),), -0.2, 0.2)), 2.0345052689663135e-05, 0.05)
    skip_gain = normal_values(streams_of[5], (D,), 1.0, 4.0, ((0, 16),), jnp.float32)
    return {"tokens": tokens, "in_weight": in_weight, "short_taps": short_taps, "residues": residues, "decay_rates": decay_rates, "skip_gain": skip_gain}


def reference(tokens, in_weight, short_taps, residues, decay_rates, skip_gain):
    flat_weight = in_weight.reshape(D, 3 * D)
    projected = jnp.dot(tokens, flat_weight, preferred_element_type=jnp.float32)
    projected = projected.reshape(TOKENS, 3, D).astype(jnp.bfloat16)
    padded = jnp.concatenate([jnp.zeros((TAPS - 1, 3, D), jnp.bfloat16), projected], axis=0).astype(jnp.float32)
    featured = jnp.zeros((TOKENS, 3, D), jnp.float32)
    for shift in range(TAPS):
        featured = featured + short_taps[:, shift, :] * padded[TAPS - 1 - shift:TAPS - 1 - shift + TOKENS]
    query = featured[:, 0]
    gated = (featured[:, 1] * featured[:, 2]).astype(jnp.bfloat16)
    values = gated.astype(jnp.float32)
    nblocks = TOKENS // BLOCK
    blocks = values.reshape(nblocks, BLOCK, D)
    lags = jnp.arange(BLOCK, dtype=jnp.float32)
    offsets = lags[:, None] - lags[None, :]
    causal = offsets >= 0
    spans = jnp.maximum(offsets, 0.0)[:, :, None]
    toeplitz = jnp.zeros((BLOCK, BLOCK, D), jnp.float32)
    for mode in range(POLES):
        toeplitz = toeplitz + residues[mode] * jnp.exp(-decay_rates[mode] * spans)
    toeplitz = jnp.where(causal[:, :, None], toeplitz, 0.0)
    inner = jnp.einsum('ijc,bjc->bic', toeplitz, blocks, precision=lax.Precision.HIGHEST)
    tails = jnp.exp(-decay_rates[None] * (BLOCK - 1 - lags)[:, None, None])
    ends = jnp.einsum('jnc,bjc->bnc', tails, blocks, precision=lax.Precision.HIGHEST)
    step_decay = jnp.exp(-decay_rates * BLOCK)

    def advance(state, block_end):
        return step_decay * state + block_end, state

    final, entering = lax.scan(advance, jnp.zeros((POLES, D), jnp.float32), ends)
    leads = residues[None] * jnp.exp(-decay_rates[None] * (lags + 1.0)[:, None, None])
    across = jnp.einsum('inc,bnc->bic', leads, entering, precision=lax.Precision.HIGHEST)
    conv = (inner + across).reshape(TOKENS, D)
    return (query * (conv + skip_gain * values)).astype(jnp.bfloat16)
```

```python
import functools

import jax
import jax.numpy as jnp
from jax import lax
from jax.experimental import pallas as pl
from jax.experimental.pallas import tpu as pltpu
from jax.sharding import PartitionSpec as P

MESH = pl.DeviceIdType.MESH
F32 = jnp.float32
BF16 = jnp.bfloat16
L = 16
GROUP = 8 * L
HALO = 8
CHUNKS = ((1408, 128), (0, 256), (256, 256), (512, 256), (768, 256), (1024, 256), (1280, 128))


def kernel(
    tokens, weight, taps, residues, decay, skip, out,
    tok, w, proj, query, base, states, mixed, carry, lam, filt, scan, bdec, gdec, lead, tapb, skipb,
    final, landed, entry,
    s_send, s_recv, w_send_sem, w_recv_sem, h_send, h_recv, f_send, f_recv, local,
):
    ch, ctx = lax.axis_index("ch"), lax.axis_index("ctx")
    x, y, z, core = ch // 4, ch % 4, ctx // 2, ctx % 2
    sibling = z * 2 + 1 - core
    rows = tokens.shape[0]
    poles = residues.shape[0]
    groups = rows // GROUP
    nctx = 16

    def near(axis, d):
        return {"ch": (x + d) % 4 * 4 + y if axis == "x" else x * 4 + (y + d) % 4}

    own_tok = pltpu.make_async_copy(tokens, tok.at[x, y], local.at[0])
    own_w = pltpu.make_async_copy(weight, w.at[pl.ds(ctx * 256, 256)], local.at[1])
    own_tok.start()
    own_w.start()
    barrier = pltpu.get_barrier_semaphore()
    for axis in "xy":
        for d in (1, 3):
            pl.semaphore_signal(barrier, 1, device_id=near(axis, d), device_id_type=MESH)
    for o in range(1, nctx):
        pl.semaphore_signal(barrier, 1, device_id={"ctx": (ctx + o) % nctx}, device_id_type=MESH)
    pl.semaphore_wait(barrier, 4 + nctx - 1)
    own_tok.wait()
    own_w.wait()

    sent = []
    copies = {}

    def send(key, ref, to, ss, rs):
        copy = pltpu.make_async_remote_copy(
            src_ref=ref, dst_ref=ref, send_sem=ss, recv_sem=rs, device_id=to, device_id_type=MESH
        )
        copy.start()
        sent.append(copy)
        copies[key] = copy

    def halves(r):
        first, size = CHUNKS[r]
        return (("x", "y", first, size // 2, 0), ("y", "x", first + size // 2, size // 2, 1))

    def stage(r, number, forward):
        for one, two, first, size, h in halves(r):
            axis = one if number == 1 else two
            for i, d in enumerate((1, 3)):
                k = (number - 1) * 8 + forward * 4 + h * 2 + i
                at_x, at_y, start, count = x, y, first, size
                if forward:
                    copies[r, number, 0, h, i].wait_recv()
                    if axis == "x":
                        at_x = (x - d) % 4
                    else:
                        at_y = (y - d) % 4
                    start, count = first + i * (size // 2), size // 2
                span = pl.ds(start, count)
                if number == 1:
                    ref = tok.at[at_x, at_y, span]
                elif axis == "x":
                    ref = tok.at[at_x, :, span]
                else:
                    ref = tok.at[:, at_y, span]
                send((r, number, forward, h, i), ref, near(axis, d), s_send.at[r, k], s_recv.at[r, k])

    def landed_stage(r, number):
        for h in (0, 1):
            for i in (0, 1):
                copies[r, number, 1, h, i].wait_recv()

    def weights(s):
        for i, d in enumerate((1, 7)):
            owner = (z - d * s) % 8 * 2 + core
            for part in (0, 1):
                if s > 0:
                    if s == 4 and part != i:
                        continue
                    copies["w", s - 1, i, part].wait_recv()
                ref = w.at[pl.ds(owner * 256 + part * 128, 128)]
                if s < 3 or (s == 3 and part == i):
                    to = {"ctx": (z + d) % 8 * 2 + core}
                    send(("w", s, i, part), ref, to, w_send_sem.at[s, i, part], w_recv_sem.at[s, i, part])
                if s > 0 or i == 0:
                    send(
                        ("s", s, i, part), ref, {"ctx": sibling},
                        w_send_sem.at[s, 2 + i, part], w_recv_sem.at[s, 2 + i, part],
                    )

    def tables():
        ids = lax.broadcasted_iota(jnp.int32, (8, 128), 0)
        lanes8 = ids.astype(F32)
        for t in (0, 1):
            cols = pl.ds(t * 128, 128)
            for g in range(3):
                for k in range(3):
                    tapb[t, g * 3 + k] = jnp.broadcast_to(taps[g, k : k + 1, cols], (8, 128))
            skipb[t] = jnp.broadcast_to(skip[:, cols], (8, 128))
            for m in range(L):
                filt[t, m] = jnp.zeros((8, 128), F32)
            for n in range(poles):
                lam[t, n] = jnp.broadcast_to(decay[n : n + 1, cols], (8, 128))
                lead[t, n] = jnp.broadcast_to(residues[n : n + 1, cols], (8, 128))

            def mode(n, _):
                rate, gain = lam[t, n], lead[t, n]
                step = jnp.exp(-rate)
                lam[t, n] = step
                lead[t, n] = gain * step
                for k, s in enumerate((1, 2, 4)):
                    scan[t, k, n] = jnp.where(ids >= s, jnp.exp(-rate * float(L * s)), 0.0)
                bdec[t, n] = jnp.exp(-rate * (lanes8 * float(L)))
                gdec[t, n] = jnp.exp(-rate * float(GROUP))
                carry[t, n] = jnp.zeros((8, 128), F32)
                for m in range(L):
                    filt[t, m] += gain * jnp.exp(-rate * float(m))
                return 0

            lax.fori_loop(0, poles, mode, 0)

    def project(first, size):
        span = pl.ds(first, size)
        left = jnp.concatenate([tok[i // 4, i % 4, span, :] for i in range(16)], axis=1)
        for g in range(3):
            total = jnp.dot(left, w[:, g * 256 : (g + 1) * 256], preferred_element_type=F32)
            total = total.astype(BF16).astype(F32)
            for t in (0, 1):
                proj[g * 2 + t, pl.ds(HALO + first, size), :] = total[:, t * 128 : (t + 1) * 128]

    def filter_group(g, t):
        first = HALO + g * GROUP
        ids = lax.broadcasted_iota(jnp.int32, (8, 128), 0)

        def rows_at(part, i):
            return proj[part * 2 + t, pl.ds(first + i, 8, stride=L), :]

        feats = []
        for part in range(3):
            k0, k1, k2 = (tapb[t, part * 3 + k] for k in range(3))
            two, one = rows_at(part, -2), rows_at(part, -1)
            listed = []
            for i in range(L):
                now = rows_at(part, i)
                value = k0 * now + k1 * one + k2 * two
                if part == 0:
                    query[g, t, i] = value
                else:
                    listed.append(value)
                two, one = one, now
            feats.append(listed)
        gated = [(a * b).astype(BF16).astype(F32) for a, b in zip(feats[1], feats[2])]

        for n in range(poles):
            step = lam[t, n]
            end = gated[0]
            for i in range(1, L):
                end = step * end + gated[i]
            for k, s in enumerate((1, 2, 4)):
                end = end + scan[t, k, n] * pltpu.roll(end, s, axis=0)
            before = jnp.where(ids >= 1, pltpu.roll(end, 1, axis=0), 0.0)
            held = carry[t, n]
            states[g, t, n] = before + bdec[t, n] * held
            carry[t, n] = jnp.broadcast_to(end[7:8], (8, 128)) + gdec[t, n] * held

        for i in range(L):
            total = skipb[t] * gated[i]
            for j in range(i + 1):
                total = total + filt[t, i - j] * gated[j]
            base[g, t, i] = total

    def filter_groups(lo, hi):
        def step(k, _):
            filter_group(lo + k // 2, k % 2)
            return 0

        lax.fori_loop(0, 2 * (hi - lo), step, 0)

    def finish(k, _):
        g, t = k // 2, k % 2
        flow = []
        for n in range(poles):
            held = entry[t, n]
            flow.append(lead[t, n] * (states[g, t, n] + bdec[t, n] * held))
            entry[t, n] = gdec[t, n] * held
        steps = [lam[t, n] for n in range(poles)]
        for i in range(L):
            parts = flow
            while len(parts) > 1:
                parts = [a + b for a, b in zip(parts[::2], parts[1::2])]
            mixed[t, pl.ds(g * GROUP + i, 8, stride=L), :] = query[g, t, i] * (base[g, t, i] + parts[0])
            if i < L - 1:
                flow = [a * b for a, b in zip(flow, steps)]
        span = pl.ds(pl.multiple_of(g * GROUP, GROUP), GROUP)
        out[span, pl.ds(pl.multiple_of(t * 128, 128), 128)] = mixed[t, span, :].astype(BF16)
        return 0

    count = len(CHUNKS)
    weights(0)
    for r in range(count):
        stage(r, 1, 0)
    tables()
    for r in range(count):
        stage(r, 1, 1)
    weights(1)
    landed_stage(0, 1)
    stage(0, 2, 0)
    landed_stage(1, 1)
    stage(1, 2, 0)
    for r in range(2, count):
        landed_stage(r, 1)

    def tick(r):
        stage(r, 2, 1)
        if r + 2 < count:
            stage(r + 2, 2, 0)

    def compute(r):
        landed_stage(r, 2)
        first, size = CHUNKS[r]
        if size == 128:
            project(first, size)
        else:
            for half in range(0, size, 256):
                project(first + half, 256)

    tick(0)
    weights(2)
    tick(1)
    weights(3)
    tick(2)
    weights(4)
    for key, copy in copies.items():
        if key[0] == "s":
            copy.wait_recv()
    compute(0)
    halo = pltpu.make_async_remote_copy(
        src_ref=proj.at[:, pl.ds(rows, HALO)], dst_ref=proj.at[:, pl.ds(0, HALO)],
        send_sem=h_send, recv_sem=h_recv,
        device_id={"ctx": (ctx + 1) % nctx}, device_id_type=MESH,
    )

    @pl.when(ctx == 0)
    def _():
        proj[:, pl.ds(0, HALO), :] = jnp.zeros((6, HALO, 128), F32)

    @pl.when(ctx < nctx - 1)
    def _():
        halo.start()

    compute(1)

    @pl.when(ctx > 0)
    def _():
        halo.wait_recv()

    filter_groups(0, 2)
    tick(3)
    compute(2)
    filter_groups(2, 4)
    tick(4)
    compute(3)
    filter_groups(4, 6)
    tick(5)
    compute(4)
    filter_groups(6, 8)
    tick(6)
    compute(5)
    filter_groups(8, 10)
    compute(6)
    filter_groups(10, 12)

    for t in (0, 1):
        for n in range(poles):
            final[n : n + 1, t * 128 : (t + 1) * 128] = carry[t, n, 0:1, :]

    def exchange(o):
        return pltpu.make_async_remote_copy(
            src_ref=final, dst_ref=landed.at[ctx],
            send_sem=f_send.at[o], recv_sem=f_recv.at[o],
            device_id={"ctx": (ctx + o) % nctx}, device_id_type=MESH,
        )

    for o in range(1, nctx):

        @pl.when(ctx + o < nctx)
        def _():
            exchange(o).start()

    for o in range(1, nctx):

        @pl.when(ctx >= o)
        def _():
            pltpu.make_async_remote_copy(
                src_ref=final, dst_ref=landed.at[(ctx - o) % nctx],
                send_sem=f_send.at[o], recv_sem=f_recv.at[o],
                device_id={"ctx": (ctx + o) % nctx}, device_id_type=MESH,
            ).wait_recv()

    across = jnp.exp(-decay[...] * float(rows))

    def join(k, total):
        return across * total + landed[k]

    incoming = lax.fori_loop(0, ctx, join, jnp.zeros((poles, 256), F32))
    for t in (0, 1):
        for n in range(poles):
            entry[t, n] = jnp.broadcast_to(incoming[n : n + 1, t * 128 : (t + 1) * 128], (8, 128))
    lax.fori_loop(0, 2 * groups, finish, 0)

    for copy in sent:
        copy.wait_send()

    @pl.when(ctx < nctx - 1)
    def _():
        halo.wait_send()

    for o in range(1, nctx):

        @pl.when(ctx + o < nctx)
        def _():
            exchange(o).wait_send()


def body(tokens, in_weight, short_taps, residues, decay_rates, skip_gain):
    rows, poles = tokens.shape[0], residues.shape[0]
    groups = rows // GROUP
    flops = 2 * rows * 4096 * 768
    dma = pltpu.SemaphoreType.DMA
    vmem, anywhere = pl.BlockSpec(memory_space=pltpu.VMEM), pl.BlockSpec(memory_space=pl.ANY)
    return pl.pallas_call(
        kernel,
        out_shape=jax.ShapeDtypeStruct((rows, 256), BF16),
        in_specs=[anywhere, anywhere, vmem, vmem, vmem, vmem],
        out_specs=vmem,
        scratch_shapes=[
            pltpu.VMEM((4, 4, rows, 256), BF16),
            pltpu.VMEM((4096, 768), BF16),
            pltpu.VMEM((6, HALO + rows, 128), F32),
            pltpu.VMEM((groups, 2, L, 8, 128), F32),
            pltpu.VMEM((groups, 2, L, 8, 128), F32),
            pltpu.VMEM((groups, 2, poles, 8, 128), F32),
            pltpu.VMEM((2, rows, 128), F32),
            pltpu.VMEM((2, poles, 8, 128), F32),
            pltpu.VMEM((2, poles, 8, 128), F32),
            pltpu.VMEM((2, L, 8, 128), F32),
            pltpu.VMEM((2, 3, poles, 8, 128), F32),
            pltpu.VMEM((2, poles, 8, 128), F32),
            pltpu.VMEM((2, poles, 8, 128), F32),
            pltpu.VMEM((2, poles, 8, 128), F32),
            pltpu.VMEM((2, 9, 8, 128), F32),
            pltpu.VMEM((2, 8, 128), F32),
            pltpu.VMEM((poles, 256), F32),
            pltpu.VMEM((16, poles, 256), F32),
            pltpu.VMEM((2, poles, 8, 128), F32),
            dma((len(CHUNKS), 16)),
            dma((len(CHUNKS), 16)),
            dma((5, 4, 2)),
            dma((5, 4, 2)),
            dma(()),
            dma(()),
            dma((16,)),
            dma((16,)),
            dma((2,)),
        ],
        compiler_params=pltpu.CompilerParams(
            collective_id=0, has_side_effects=True, vmem_limit_bytes=56 * 2**20
        ),
        cost_estimate=pl.CostEstimate(flops=flops, bytes_accessed=4 * 2**20, transcendentals=0),
    )(tokens, in_weight.reshape(256, 768), short_taps, residues, decay_rates, skip_gain.reshape(1, 256))


def solution(mesh):
    in_specs = (
        P("ctx", "ch"),
        P("ctx", None, "ch"),
        P(None, None, "ch"),
        P(None, "ch"),
        P(None, "ch"),
        P("ch"),
    )
    return jax.shard_map(body, mesh=mesh, in_specs=in_specs, out_specs=P("ctx", "ch"), check_vma=False)
```

```python
import functools

import jax
import jax.numpy as jnp
from jax import lax
from jax.experimental import pallas as pl
from jax.experimental.pallas import tpu as pltpu
from jax.sharding import PartitionSpec as P

MESH = pl.DeviceIdType.MESH
F32 = jnp.float32
BF16 = jnp.bfloat16
L = 16
GROUP = 8 * L
HALO = 8
CHUNKS = ((1408, 128), (0, 256), (256, 256), (512, 256), (768, 256), (1024, 256), (1280, 128))


def kernel(
    tokens, weight, taps_in, residues_in, decay_in, skip_in, out,
    taps, residues, decay, skip, tok, w, proj, query, base, states, mixed, carry, lam, filt, scan, bdec, gdec, lead, tapb, skipb,
    final, landed, entry,
    s_send, s_recv, w_send_sem, w_recv_sem, h_send, h_recv, f_send, f_recv, local,
):
    ch, ctx = lax.axis_index("ch"), lax.axis_index("ctx")
    x, y, z, core = ch // 4, ch % 4, ctx // 2, ctx % 2
    sibling = z * 2 + 1 - core
    rows = tokens.shape[0]
    poles = residues_in.shape[0]
    groups = rows // GROUP
    nctx = 16

    def near(axis, d):
        return {"ch": (x + d) % 4 * 4 + y if axis == "x" else x * 4 + (y + d) % 4}

    own_tok = pltpu.make_async_copy(tokens, tok.at[x, y], local.at[0])
    own_w = pltpu.make_async_copy(weight, w.at[:, pl.ds(ctx * 256, 256)], local.at[1])
    own_tok.start()
    own_w.start()
    small = [
        pltpu.make_async_copy(src, dst, local.at[2 + i])
        for i, (src, dst) in enumerate(
            ((taps_in, taps), (residues_in, residues), (decay_in, decay), (skip_in, skip))
        )
    ]
    for copy in small:
        copy.start()
    barrier = pltpu.get_barrier_semaphore()
    for axis in "xy":
        for d in (1, 3):
            pl.semaphore_signal(barrier, 1, device_id=near(axis, d), device_id_type=MESH)
    for o in (1, 2, nctx - 2, nctx - 1):
        pl.semaphore_signal(barrier, 1, device_id={"ctx": (ctx + o) % nctx}, device_id_type=MESH)
    pl.semaphore_wait(barrier, 8)
    own_tok.wait()
    own_w.wait()

    sent = []
    copies = {}

    def send(key, ref, to, ss, rs):
        copy = pltpu.make_async_remote_copy(
            src_ref=ref, dst_ref=ref, send_sem=ss, recv_sem=rs, device_id=to, device_id_type=MESH
        )
        copy.start()
        sent.append(copy)
        copies[key] = copy

    def halves(r):
        first, size = CHUNKS[r]
        return (("x", "y", first, size // 2, 0), ("y", "x", first + size // 2, size // 2, 1))

    def stage(r, number, forward):
        for one, two, first, size, h in halves(r):
            axis = one if number == 1 else two
            for i, d in enumerate((1, 3)):
                k = (number - 1) * 8 + forward * 4 + h * 2 + i
                at_x, at_y, start, count = x, y, first, size
                if forward:
                    copies[r, number, 0, h, i].wait_recv()
                    if axis == "x":
                        at_x = (x - d) % 4
                    else:
                        at_y = (y - d) % 4
                    start, count = first + i * (size // 2), size // 2
                span = pl.ds(start, count)
                if number == 1:
                    ref = tok.at[at_x, at_y, span]
                elif axis == "x":
                    ref = tok.at[at_x, :, span]
                else:
                    ref = tok.at[:, at_y, span]
                send((r, number, forward, h, i), ref, near(axis, d), s_send.at[r, k], s_recv.at[r, k])

    def landed_stage(r, number):
        for h in (0, 1):
            for i in (0, 1):
                copies[r, number, 1, h, i].wait_recv()

    def weights(s):
        for i, d in enumerate((1, 7)):
            owner = (z - d * s) % 8 * 2 + core
            for part in (0, 1):
                if s > 0:
                    if s == 4 and part != i:
                        continue
                    copies["w", s - 1, i, part].wait_recv()
                ref = w.at[:, pl.ds(owner * 256 + part * 128, 128)]
                if s < 3 or (s == 3 and part == i):
                    to = {"ctx": (z + d) % 8 * 2 + core}
                    send(("w", s, i, part), ref, to, w_send_sem.at[s, i, part], w_recv_sem.at[s, i, part])
                if s > 0 or i == 0:
                    send(
                        ("s", s, i, part), ref, {"ctx": sibling},
                        w_send_sem.at[s, 2 + i, part], w_recv_sem.at[s, 2 + i, part],
                    )

    def tables(t):
        ids = lax.broadcasted_iota(jnp.int32, (8, 128), 0)
        lanes8 = ids.astype(F32)
        cols = pl.ds(t * 128, 128)
        for g in range(3):
            for k in range(3):
                tapb[t, g * 3 + k] = jnp.broadcast_to(taps[g, k : k + 1, cols], (8, 128))
        skipb[t] = jnp.broadcast_to(skip[:, cols], (8, 128))
        for m in range(L):
            filt[t, m] = jnp.zeros((8, 128), F32)
        for n in range(poles):
            lam[t, n] = jnp.broadcast_to(decay[n : n + 1, cols], (8, 128))
            lead[t, n] = jnp.broadcast_to(residues[n : n + 1, cols], (8, 128))

        def mode(n, _):
            rate, gain = lam[t, n], lead[t, n]
            step = jnp.exp(-rate)
            lam[t, n] = step
            lead[t, n] = gain * step
            for k, s in enumerate((1, 2, 4)):
                scan[t, k, n] = jnp.where(ids >= s, jnp.exp(-rate * float(L * s)), 0.0)
            bdec[t, n] = jnp.exp(-rate * (lanes8 * float(L)))
            gdec[t, n] = jnp.exp(-rate * float(GROUP))
            carry[t, n] = jnp.zeros((8, 128), F32)
            for m in range(L):
                filt[t, m] += gain * jnp.exp(-rate * float(m))
            return 0

        lax.fori_loop(0, poles, mode, 0)

    def project(first, size):
        span = pl.ds(first, size)
        left = jnp.concatenate([tok[i // 4, i % 4, span, :] for i in range(16)], axis=1)
        for g in range(3):
            total = jnp.dot(left, w[g], preferred_element_type=F32)
            total = total.astype(BF16).astype(F32)
            for t in (0, 1):
                proj[g * 2 + t, pl.ds(HALO + first, size), :] = total[:, t * 128 : (t + 1) * 128]

    def filter_group(g, t, convolve):
        first = HALO + g * GROUP
        ids = lax.broadcasted_iota(jnp.int32, (8, 128), 0)

        def rows_at(part, i):
            return proj[part * 2 + t, pl.ds(first + i, 8, stride=L), :]

        feats = []
        for part in range(3):
            k0, k1, k2 = (tapb[t, part * 3 + k] for k in range(3))
            two, one = rows_at(part, -2), rows_at(part, -1)
            listed = []
            for i in range(L):
                now = rows_at(part, i)
                value = k0 * now + k1 * one + k2 * two
                if part == 0:
                    query[g, t, i] = value
                else:
                    listed.append(value)
                two, one = one, now
            feats.append(listed)
        gated = [(a * b).astype(BF16).astype(F32) for a, b in zip(feats[1], feats[2])]

        for n in range(poles):
            step = lam[t, n]
            end = gated[0]
            for i in range(1, L):
                end = step * end + gated[i]
            for k, s in enumerate((1, 2, 4)):
                end = end + scan[t, k, n] * pltpu.roll(end, s, axis=0)
            before = jnp.where(ids >= 1, pltpu.roll(end, 1, axis=0), 0.0)
            held = carry[t, n]
            states[g, t, n] = before + bdec[t, n] * held
            carry[t, n] = jnp.broadcast_to(end[7:8], (8, 128)) + gdec[t, n] * held

        if convolve:
            convolve_group(g, t, gated)
        else:
            for i in range(L):
                base[g, t, i] = gated[i]

    def convolve_group(g, t, gated):
        for i in range(L):
            total = skipb[t] * gated[i]
            for j in range(i + 1):
                total = total + filt[t, i - j] * gated[j]
            base[g, t, i] = total

    def filter_groups(lo, hi, convolve=True):
        def step(k, _):
            filter_group(lo + k // 2, k % 2, convolve)
            return 0

        lax.fori_loop(0, 2 * (hi - lo), step, 0)

    def convolve_groups(lo, hi):
        def step(k, _):
            g, t = lo + k // 2, k % 2
            convolve_group(g, t, [base[g, t, i] for i in range(L)])
            return 0

        lax.fori_loop(0, 2 * (hi - lo), step, 0)

    def finish(g, _):
        span = pl.ds(pl.multiple_of(g * GROUP, GROUP), GROUP)
        for t in (0, 1):
            flow = []
            for n in range(poles):
                held = entry[t, n]
                flow.append(lead[t, n] * (states[g, t, n] + bdec[t, n] * held))
                entry[t, n] = gdec[t, n] * held
            for i in range(L):
                parts = flow
                while len(parts) > 1:
                    parts = [a + b for a, b in zip(parts[::2], parts[1::2])]
                mixed[t, pl.ds(g * GROUP + i, 8, stride=L), :] = query[g, t, i] * (base[g, t, i] + parts[0])
                if i < L - 1:
                    flow = [a * lam[t, n] for n, a in enumerate(flow)]
            out[span, t * 128 : (t + 1) * 128] = mixed[t, span, :].astype(BF16)
        return 0

    count = len(CHUNKS)
    weights(0)
    for r in range(count):
        stage(r, 1, 0)
    for r in range(count):
        stage(r, 1, 1)
    weights(1)
    landed_stage(0, 1)
    stage(0, 2, 0)
    landed_stage(1, 1)
    stage(1, 2, 0)
    for r in range(2, count):
        landed_stage(r, 1)

    def tick(r):
        stage(r, 2, 1)
        if r + 2 < count:
            stage(r + 2, 2, 0)

    def compute(r):
        landed_stage(r, 2)
        project(*CHUNKS[r])

    for copy in small:
        copy.wait()
    tables(0)
    tick(0)
    tables(1)
    weights(2)
    tick(1)
    weights(3)
    tick(2)
    weights(4)
    for key, copy in copies.items():
        if key[0] == "s":
            copy.wait_recv()
    compute(0)
    halo = pltpu.make_async_remote_copy(
        src_ref=proj.at[:, pl.ds(rows, HALO)], dst_ref=proj.at[:, pl.ds(0, HALO)],
        send_sem=h_send, recv_sem=h_recv,
        device_id={"ctx": (ctx + 1) % nctx}, device_id_type=MESH,
    )

    @pl.when(ctx == 0)
    def _():
        proj[:, pl.ds(0, HALO), :] = jnp.zeros((6, HALO, 128), F32)

    @pl.when(ctx < nctx - 1)
    def _():
        halo.start()

    tick(3)
    compute(1)
    compute(2)

    @pl.when(ctx > 0)
    def _():
        halo.wait_recv()

    filter_groups(0, 4)
    tick(4)
    compute(3)
    filter_groups(4, 6)
    tick(5)
    compute(4)
    filter_groups(6, 8)
    tick(6)
    compute(5)
    filter_groups(8, 10)
    compute(6)
    filter_groups(10, 12, False)

    for t in (0, 1):
        held = jnp.concatenate([carry[t, n, 0:1, :] for n in range(poles)], axis=0)
        final[:, t * 128 : (t + 1) * 128] = held.astype(BF16)

    def exchange(o):
        return pltpu.make_async_remote_copy(
            src_ref=final, dst_ref=landed.at[ctx],
            send_sem=f_send.at[o], recv_sem=f_recv.at[o],
            device_id={"ctx": (ctx + o) % nctx}, device_id_type=MESH,
        )

    for o in range(1, nctx):

        @pl.when(ctx + o < nctx)
        def _():
            exchange(o).start()

    convolve_groups(10, 12)
    for o in range(1, nctx):

        @pl.when(ctx >= o)
        def _():
            pltpu.make_async_remote_copy(
                src_ref=final, dst_ref=landed.at[(ctx - o) % nctx],
                send_sem=f_send.at[o], recv_sem=f_recv.at[o],
                device_id={"ctx": (ctx + o) % nctx}, device_id_type=MESH,
            ).wait_recv()

    across = jnp.exp(-decay[...] * float(rows))

    def join(k, total):
        return across * total + landed[k].astype(F32)

    incoming = lax.fori_loop(0, ctx, join, jnp.zeros((poles, 256), F32))
    for t in (0, 1):
        for n in range(poles):
            entry[t, n] = jnp.broadcast_to(incoming[n : n + 1, t * 128 : (t + 1) * 128], (8, 128))
    lax.fori_loop(0, groups, finish, 0)

    for copy in sent:
        copy.wait_send()

    @pl.when(ctx < nctx - 1)
    def _():
        halo.wait_send()

    for o in range(1, nctx):

        @pl.when(ctx + o < nctx)
        def _():
            exchange(o).wait_send()


def body(tokens, in_weight, short_taps, residues, decay_rates, skip_gain):
    rows, poles = tokens.shape[0], residues.shape[0]
    groups = rows // GROUP
    flops = 2 * rows * 4096 * 768
    dma = pltpu.SemaphoreType.DMA
    anywhere = pl.BlockSpec(memory_space=pl.ANY)
    return pl.pallas_call(
        kernel,
        out_shape=pltpu.VMEM((rows, 256), BF16),
        in_specs=[anywhere] * 6,
        out_specs=pl.BlockSpec(memory_space=pltpu.VMEM),
        scratch_shapes=[
            pltpu.VMEM((3, 3, 256), F32),
            pltpu.VMEM((poles, 256), F32),
            pltpu.VMEM((poles, 256), F32),
            pltpu.VMEM((1, 256), F32),
            pltpu.VMEM((4, 4, rows, 256), BF16),
            pltpu.VMEM((3, 4096, 256), BF16),
            pltpu.VMEM((6, HALO + rows, 128), F32),
            pltpu.VMEM((groups, 2, L, 8, 128), F32),
            pltpu.VMEM((groups, 2, L, 8, 128), F32),
            pltpu.VMEM((groups, 2, poles, 8, 128), F32),
            pltpu.VMEM((2, rows, 128), F32),
            pltpu.VMEM((2, poles, 8, 128), F32),
            pltpu.VMEM((2, poles, 8, 128), F32),
            pltpu.VMEM((2, L, 8, 128), F32),
            pltpu.VMEM((2, 3, poles, 8, 128), F32),
            pltpu.VMEM((2, poles, 8, 128), F32),
            pltpu.VMEM((2, poles, 8, 128), F32),
            pltpu.VMEM((2, poles, 8, 128), F32),
            pltpu.VMEM((2, 9, 8, 128), F32),
            pltpu.VMEM((2, 8, 128), F32),
            pltpu.VMEM((poles, 256), BF16),
            pltpu.VMEM((16, poles, 256), BF16),
            pltpu.VMEM((2, poles, 8, 128), F32),
            dma((len(CHUNKS), 16)),
            dma((len(CHUNKS), 16)),
            dma((5, 4, 2)),
            dma((5, 4, 2)),
            dma(()),
            dma(()),
            dma((16,)),
            dma((16,)),
            dma((6,)),
        ],
        compiler_params=pltpu.CompilerParams(
            collective_id=0, has_side_effects=True, vmem_limit_bytes=56 * 2**20
        ),
        cost_estimate=pl.CostEstimate(flops=flops, bytes_accessed=4 * 2**20, transcendentals=0),
    )(tokens, in_weight.transpose(1, 0, 2), short_taps, residues, decay_rates, skip_gain.reshape(1, 256))


def solution(mesh):
    in_specs = (
        P("ctx", "ch"),
        P("ctx", None, "ch"),
        P(None, None, "ch"),
        P(None, "ch"),
        P(None, "ch"),
        P("ch"),
    )
    return jax.shard_map(body, mesh=mesh, in_specs=in_specs, out_specs=P("ctx", "ch"), check_vma=False)
```

```python
import functools

import jax
import jax.numpy as jnp
from jax import lax
from jax.experimental import pallas as pl
from jax.experimental.pallas import tpu as pltpu
from jax.sharding import PartitionSpec as P

MESH = pl.DeviceIdType.MESH
F32 = jnp.float32
BF16 = jnp.bfloat16
L = 16
GROUP = 8 * L
HALO = 8
LATE = 1024
CHUNKS = ((1408, 128), (0, 384), (384, 384), (768, 256), (1024, 256), (1280, 128))


def kernel(
    tokens, weight, taps_in, residues_in, decay_in, skip_in, out,
    taps, residues, decay, skip, tok, w, proj, query, base, states, mixed, carry, lam, filt, scan, bdec, gdec, lead, tapb, skipb,
    final, landed, entry, partial,
    s_send, s_recv, w_send_sem, w_recv_sem, h_send, h_recv, f_send, f_recv, local,
):
    ch, ctx = lax.axis_index("ch"), lax.axis_index("ctx")
    x, y, z, core = ch // 4, ch % 4, ctx // 2, ctx % 2
    sibling = z * 2 + 1 - core
    rows = tokens.shape[0]
    poles = residues_in.shape[0]
    groups = rows // GROUP
    nctx = 16

    def near(axis, d):
        return {"ch": (x + d) % 4 * 4 + y if axis == "x" else x * 4 + (y + d) % 4}

    barrier = pltpu.get_barrier_semaphore()
    for axis in "xy":
        for d in (1, 3):
            pl.semaphore_signal(barrier, 1, device_id=near(axis, d), device_id_type=MESH)
    for o in (1, 2, nctx - 2, nctx - 1):
        pl.semaphore_signal(barrier, 1, device_id={"ctx": (ctx + o) % nctx}, device_id_type=MESH)
    own_tok = pltpu.make_async_copy(tokens, tok.at[x, y], local.at[0])
    own_w = pltpu.make_async_copy(weight, w.at[:, pl.ds(ctx * 256, 256)], local.at[1])
    own_tok.start()
    own_w.start()
    small = [
        pltpu.make_async_copy(src, dst, local.at[2 + i])
        for i, (src, dst) in enumerate(
            ((taps_in, taps), (residues_in, residues), (decay_in, decay), (skip_in, skip))
        )
    ]
    for copy in small:
        copy.start()
    pl.semaphore_wait(barrier, 8)
    own_tok.wait()
    own_w.wait()

    sent = []
    copies = {}

    def send(key, ref, to, ss, rs):
        copy = pltpu.make_async_remote_copy(
            src_ref=ref, dst_ref=ref, send_sem=ss, recv_sem=rs, device_id=to, device_id_type=MESH
        )
        copy.start()
        sent.append(copy)
        copies[key] = copy

    def halves(r):
        first, size = CHUNKS[r]
        return (("x", "y", first, size // 2, 0), ("y", "x", first + size // 2, size // 2, 1))

    def stage(r, number, forward):
        for one, two, first, size, h in halves(r):
            axis = one if number == 1 else two
            for i, d in enumerate((1, 3)):
                k = (number - 1) * 8 + forward * 4 + h * 2 + i
                at_x, at_y, start, count = x, y, first, size
                if forward:
                    copies[r, number, 0, h, i].wait_recv()
                    if axis == "x":
                        at_x = (x - d) % 4
                    else:
                        at_y = (y - d) % 4
                    start, count = first + i * (size // 2), size // 2
                span = pl.ds(start, count)
                if number == 1:
                    ref = tok.at[at_x, at_y, span]
                elif axis == "x":
                    ref = tok.at[at_x, :, span]
                else:
                    ref = tok.at[:, at_y, span]
                send((r, number, forward, h, i), ref, near(axis, d), s_send.at[r, k], s_recv.at[r, k])

    def landed_stage(r, number):
        for h in (0, 1):
            for i in (0, 1):
                copies[r, number, 1, h, i].wait_recv()

    def weights(s):
        for i, d in enumerate((1, 7)):
            owner = (z - d * s) % 8 * 2 + core
            for part in (0, 1):
                if s > 0:
                    if s == 4 and part != i:
                        continue
                    copies["w", s - 1, i, part].wait_recv()
                ref = w.at[:, pl.ds(owner * 256 + part * 128, 128)]
                if s < 3 or (s == 3 and part == i):
                    to = {"ctx": (z + d) % 8 * 2 + core}
                    send(("w", s, i, part), ref, to, w_send_sem.at[s, i, part], w_recv_sem.at[s, i, part])
                if s > 0 or i == 0:
                    send(
                        ("s", s, i, part), ref, {"ctx": sibling},
                        w_send_sem.at[s, 2 + i, part], w_recv_sem.at[s, 2 + i, part],
                    )

    def tables(t):
        ids = lax.broadcasted_iota(jnp.int32, (8, 128), 0)
        lanes8 = ids.astype(F32)
        cols = pl.ds(t * 128, 128)
        for g in range(3):
            for k in range(3):
                tapb[t, g * 3 + k] = jnp.broadcast_to(taps[g, k : k + 1, cols], (8, 128))
        skipb[t] = jnp.broadcast_to(skip[:, cols], (8, 128))
        for m in range(L):
            filt[t, m] = jnp.zeros((8, 128), F32)
        for n in range(poles):
            lam[t, n] = jnp.broadcast_to(decay[n : n + 1, cols], (8, 128))
            lead[t, n] = jnp.broadcast_to(residues[n : n + 1, cols], (8, 128))

        def mode(n, _):
            rate, gain = lam[t, n], lead[t, n]
            step = jnp.exp(-rate)
            lam[t, n] = step
            lead[t, n] = gain * step
            for k, s in enumerate((1, 2, 4)):
                scan[t, k, n] = jnp.where(ids >= s, jnp.exp(-rate * float(L * s)), 0.0)
            bdec[t, n] = jnp.exp(-rate * (lanes8 * float(L)))
            gdec[t, n] = jnp.exp(-rate * float(GROUP))
            carry[t, n] = jnp.zeros((8, 128), F32)
            for m in range(L):
                filt[t, m] += gain * jnp.exp(-rate * float(m))
            return 0

        lax.fori_loop(0, poles, mode, 0)

    def project(first, size, parts):
        span = pl.ds(first, size)
        left = jnp.concatenate([tok[i // 4, i % 4, span, :] for i in range(16)], axis=1)
        for g in parts:
            total = jnp.dot(left, w[g], preferred_element_type=F32)
            keep(first, size, g, total)

    def keep(first, size, part, total):
        total = total.astype(BF16).astype(F32)
        for t in (0, 1):
            proj[part * 2 + t, pl.ds(HALO + first, size), :] = total[:, t * 128 : (t + 1) * 128]

    def product(first, size, h, part, steps):
        total = None
        for k in steps:
            for i in range(4):
                at_x, at_y = (i, (y + k) % 4) if h == 0 else ((x + k) % 4, i)
                rows_of = pl.ds(pl.multiple_of((at_x * 4 + at_y) * 256, 256), 256)
                one = jnp.dot(
                    tok[at_x, at_y, pl.ds(first, size), :], w[part, rows_of, :], preferred_element_type=F32
                )
                total = one if total is None else total + one
        return total

    def begin(r):
        for _, _, first, size, h in halves(r):
            for part in range(3):
                partial[part, pl.ds(first - LATE, size), :] = product(first, size, h, part, (0, 1, 3))

    def complete(r, parts):
        for _, _, first, size, h in halves(r):
            for part in parts:
                total = partial[part, pl.ds(first - LATE, size), :] + product(first, size, h, part, (2,))
                keep(first, size, part, total)

    def features(g, t, part):
        first = HALO + g * GROUP
        k0, k1, k2 = (tapb[t, part * 3 + k] for k in range(3))
        rows_at = [proj[part * 2 + t, pl.ds(first + i, 8, stride=L), :] for i in range(-2, L)]
        return [k0 * rows_at[i + 2] + k1 * rows_at[i + 1] + k2 * rows_at[i] for i in range(L)]

    def filter_group(g, t, convolve):
        ids = lax.broadcasted_iota(jnp.int32, (8, 128), 0)
        gated = [(a * b).astype(BF16).astype(F32) for a, b in zip(features(g, t, 1), features(g, t, 2))]

        for lo in range(0, poles, 8):
            modes = range(lo, lo + 8)
            steps = [lam[t, n] for n in modes]
            held = [carry[t, n] for n in modes]
            ends = [gated[0]] * 8
            for i in range(1, L):
                ends = [a * b + gated[i] for a, b in zip(steps, ends)]
            for k, s in enumerate((1, 2, 4)):
                ends = [e + scan[t, k, n] * pltpu.roll(e, s, axis=0) for n, e in zip(modes, ends)]
            before = [jnp.where(ids >= 1, pltpu.roll(e, 1, axis=0), 0.0) for e in ends]
            for n, a, b in zip(modes, before, held):
                states[g, t, n] = a + bdec[t, n] * b
            for n, e, b in zip(modes, ends, held):
                carry[t, n] = jnp.broadcast_to(e[7:8], (8, 128)) + gdec[t, n] * b
        if convolve:
            convolve_group(g, t, gated)
        else:
            for i in range(L):
                base[g, t, i] = gated[i]

    def convolve_group(g, t, gated):
        for i, value in enumerate(features(g, t, 0)):
            query[g, t, i] = value
        taken = [filt[t, m] for m in range(L)]
        totals = [skipb[t] * a for a in gated]
        for j in range(L):
            for i in range(j, L):
                totals[i] = totals[i] + taken[i - j] * gated[j]
        for i in range(L):
            base[g, t, i] = totals[i]

    def filter_groups(lo, hi, convolve=True):
        def step(k, _):
            filter_group(lo + k // 2, k % 2, convolve)
            return 0

        lax.fori_loop(0, 2 * (hi - lo), step, 0)

    def convolve_groups(lo, hi):
        def step(k, _):
            g, t = lo + k // 2, k % 2
            convolve_group(g, t, [base[g, t, i] for i in range(L)])
            return 0

        lax.fori_loop(0, 2 * (hi - lo), step, 0)

    def finish(g, _):
        span = pl.ds(pl.multiple_of(g * GROUP, GROUP), GROUP)
        for t in (0, 1):
            flow, steps = [], [lam[t, n] for n in range(poles)]
            for n in range(poles):
                held = entry[t, n]
                flow.append(lead[t, n] * (states[g, t, n] + bdec[t, n] * held))
                entry[t, n] = gdec[t, n] * held
            for i in range(L):
                parts = flow
                while len(parts) > 1:
                    parts = [a + b for a, b in zip(parts[::2], parts[1::2])]
                mixed[t, pl.ds(g * GROUP + i, 8, stride=L), :] = query[g, t, i] * (base[g, t, i] + parts[0])
                if i < L - 1:
                    flow = [a * b for a, b in zip(flow, steps)]
            out[span, t * 128 : (t + 1) * 128] = mixed[t, span, :].astype(BF16)
        return 0

    count = len(CHUNKS)
    stage(0, 1, 0)
    weights(0)
    for r in range(1, count):
        stage(r, 1, 0)
    for r in range(count):
        stage(r, 1, 1)
    weights(1)
    landed_stage(0, 1)
    stage(0, 2, 0)
    landed_stage(1, 1)
    stage(1, 2, 0)
    for r in range(2, count):
        landed_stage(r, 1)

    def tick(r):
        stage(r, 2, 1)
        if r + 2 < count:
            stage(r + 2, 2, 0)

    def compute(r, parts=(0, 1, 2)):
        landed_stage(r, 2)
        project(*CHUNKS[r], parts)

    for copy in small:
        copy.wait()
    tables(0)
    tick(0)
    tables(1)
    weights(2)
    tick(1)
    weights(3)
    tick(2)
    weights(4)
    for key, copy in copies.items():
        if key[0] == "s":
            copy.wait_recv()
    compute(0)
    halo = pltpu.make_async_remote_copy(
        src_ref=proj.at[:, pl.ds(rows, HALO)], dst_ref=proj.at[:, pl.ds(0, HALO)],
        send_sem=h_send, recv_sem=h_recv,
        device_id={"ctx": (ctx + 1) % nctx}, device_id_type=MESH,
    )

    @pl.when(ctx == 0)
    def _():
        proj[:, pl.ds(0, HALO), :] = jnp.zeros((6, HALO, 128), F32)

    @pl.when(ctx < nctx - 1)
    def _():
        halo.start()

    compute(1)
    tick(3)

    @pl.when(ctx > 0)
    def _():
        halo.wait_recv()

    filter_groups(0, 3)
    compute(2)
    filter_groups(3, 6)
    early = len(sent)
    tick(4)
    compute(3)
    filter_groups(6, 8)
    tick(5)
    begin(4)
    for copy in sent[:early]:
        copy.wait_send()
    landed_stage(4, 2)
    complete(4, (0, 1, 2))
    filter_groups(8, 10)
    compute(5, (1, 2))
    filter_groups(10, 12, False)

    for t in (0, 1):
        final[:, t * 128 : (t + 1) * 128] = jnp.concatenate([carry[t, n, 0:1, :] for n in range(poles)], axis=0).astype(BF16)

    def exchange(o, slot):
        return pltpu.make_async_remote_copy(
            src_ref=final, dst_ref=landed.at[slot],
            send_sem=f_send.at[o], recv_sem=f_recv.at[o],
            device_id={"ctx": (ctx + o) % nctx}, device_id_type=MESH,
        )

    for o in range(nctx - 1, 0, -1):

        @pl.when(ctx + o < nctx)
        def _():
            exchange(o, ctx).start()

    project(*CHUNKS[5], (0,))
    convolve_groups(10, 12)
    for copy in sent[early:]:
        copy.wait_send()
    across = jnp.exp(-decay[...] * float(rows))
    for o in range(1, nctx):

        @pl.when(ctx >= o)
        def _():
            exchange(o, (ctx - o) % nctx).wait_recv()

    def join(k, total):
        return across * total + landed[k].astype(F32)

    incoming = lax.fori_loop(0, ctx, join, jnp.zeros((poles, 256), F32))
    for t in (0, 1):
        for n in range(poles):
            entry[t, n] = jnp.broadcast_to(incoming[n : n + 1, t * 128 : (t + 1) * 128], (8, 128))
    lax.fori_loop(0, groups, finish, 0)


    @pl.when(ctx < nctx - 1)
    def _():
        halo.wait_send()

    for o in range(1, nctx):

        @pl.when(ctx + o < nctx)
        def _():
            exchange(o, ctx).wait_send()


def body(tokens, in_weight, short_taps, residues, decay_rates, skip_gain):
    rows, poles = tokens.shape[0], residues.shape[0]
    groups = rows // GROUP
    flops = 2 * rows * 4096 * 768
    dma = pltpu.SemaphoreType.DMA
    anywhere = pl.BlockSpec(memory_space=pl.ANY)
    return pl.pallas_call(
        kernel,
        out_shape=pltpu.VMEM((rows, 256), BF16),
        in_specs=[anywhere] * 6,
        out_specs=pl.BlockSpec(memory_space=pltpu.VMEM),
        scratch_shapes=[
            pltpu.VMEM((3, 3, 256), F32),
            pltpu.VMEM((poles, 256), F32),
            pltpu.VMEM((poles, 256), F32),
            pltpu.VMEM((1, 256), F32),
            pltpu.VMEM((4, 4, rows, 256), BF16),
            pltpu.VMEM((3, 4096, 256), BF16),
            pltpu.VMEM((6, HALO + rows, 128), F32),
            pltpu.VMEM((groups, 2, L, 8, 128), F32),
            pltpu.VMEM((groups, 2, L, 8, 128), F32),
            pltpu.VMEM((groups, 2, poles, 8, 128), F32),
            pltpu.VMEM((2, rows, 128), F32),
            pltpu.VMEM((2, poles, 8, 128), F32),
            pltpu.VMEM((2, poles, 8, 128), F32),
            pltpu.VMEM((2, L, 8, 128), F32),
            pltpu.VMEM((2, 3, poles, 8, 128), F32),
            pltpu.VMEM((2, poles, 8, 128), F32),
            pltpu.VMEM((2, poles, 8, 128), F32),
            pltpu.VMEM((2, poles, 8, 128), F32),
            pltpu.VMEM((2, 9, 8, 128), F32),
            pltpu.VMEM((2, 8, 128), F32),
            pltpu.VMEM((poles, 256), BF16),
            pltpu.VMEM((16, poles, 256), BF16),
            pltpu.VMEM((2, poles, 8, 128), F32),
            pltpu.VMEM((3, 256, 256), F32),
            dma((len(CHUNKS), 16)),
            dma((len(CHUNKS), 16)),
            dma((5, 4, 2)),
            dma((5, 4, 2)),
            dma(()),
            dma(()),
            dma((16,)),
            dma((16,)),
            dma((6,)),
        ],
        compiler_params=pltpu.CompilerParams(
            collective_id=0, has_side_effects=True, vmem_limit_bytes=56 * 2**20
        ),
        cost_estimate=pl.CostEstimate(flops=flops, bytes_accessed=4 * 2**20, transcendentals=0),
    )(tokens, in_weight.transpose(1, 0, 2), short_taps, residues, decay_rates, skip_gain.reshape(1, 256))


def solution(mesh):
    in_specs = (
        P("ctx", "ch"),
        P("ctx", None, "ch"),
        P(None, None, "ch"),
        P(None, "ch"),
        P(None, "ch"),
        P("ch"),
    )
    return jax.shard_map(body, mesh=mesh, in_specs=in_specs, out_specs=P("ctx", "ch"), check_vma=False)
```

```python
import functools

import jax
import jax.numpy as jnp
from jax import lax
from jax.experimental import pallas as pl
from jax.experimental.pallas import tpu as pltpu
from jax.sharding import PartitionSpec as P

MESH = pl.DeviceIdType.MESH
F32 = jnp.float32
BF16 = jnp.bfloat16
L = 16
GROUP = 8 * L
HALO = 8
LATE = 1024
CHUNKS = ((1408, 128), (0, 640), (640, 384), (1024, 256), (1280, 128))


def kernel(
    tokens, weight, taps_in, residues_in, decay_in, skip_in, out,
    taps, residues, decay, skip, tok, w, proj, query, base, states, mixed, carry, lam, filt, scan, bdec, gdec, lead, tapb, skipb,
    final, landed, entry, partial,
    s_send, s_recv, w_send_sem, w_recv_sem, h_send, h_recv, f_send, f_recv, local,
):
    ch, ctx = lax.axis_index("ch"), lax.axis_index("ctx")
    x, y, z, core = ch // 4, ch % 4, ctx // 2, ctx % 2
    sibling = z * 2 + 1 - core
    rows = tokens.shape[0]
    poles = residues_in.shape[0]
    groups = rows // GROUP
    nctx = 16

    def near(axis, d):
        return {"ch": (x + d) % 4 * 4 + y if axis == "x" else x * 4 + (y + d) % 4}

    barrier = pltpu.get_barrier_semaphore()
    for axis in "xy":
        for d in (1, 3):
            pl.semaphore_signal(barrier, 1, device_id=near(axis, d), device_id_type=MESH)
    for o in (1, 2, nctx - 2, nctx - 1):
        pl.semaphore_signal(barrier, 1, device_id={"ctx": (ctx + o) % nctx}, device_id_type=MESH)
    own_tok = pltpu.make_async_copy(tokens, tok.at[x, y], local.at[0])
    own_w = pltpu.make_async_copy(weight, w.at[:, pl.ds(ctx * 256, 256)], local.at[1])
    own_tok.start()
    own_w.start()
    small = [
        pltpu.make_async_copy(src, dst, local.at[2 + i])
        for i, (src, dst) in enumerate(
            ((taps_in, taps), (residues_in, residues), (decay_in, decay), (skip_in, skip))
        )
    ]
    for copy in small:
        copy.start()
    pl.semaphore_wait(barrier, 8)
    own_tok.wait()
    own_w.wait()

    sent = []
    copies = {}

    def send(key, ref, to, ss, rs):
        copy = pltpu.make_async_remote_copy(
            src_ref=ref, dst_ref=ref, send_sem=ss, recv_sem=rs, device_id=to, device_id_type=MESH
        )
        copy.start()
        sent.append(copy)
        copies[key] = copy

    def halves(r):
        first, size = CHUNKS[r]
        return (("x", "y", first, size // 2, 0), ("y", "x", first + size // 2, size // 2, 1))

    def stage(r, number, forward):
        for one, two, first, size, h in halves(r):
            axis = one if number == 1 else two
            for i, d in enumerate((1, 3)):
                k = (number - 1) * 8 + forward * 4 + h * 2 + i
                at_x, at_y, start, count = x, y, first, size
                if forward:
                    copies[r, number, 0, h, i].wait_recv()
                    if axis == "x":
                        at_x = (x - d) % 4
                    else:
                        at_y = (y - d) % 4
                    start, count = first + i * (size // 2), size // 2
                span = pl.ds(start, count)
                if number == 1:
                    ref = tok.at[at_x, at_y, span]
                elif axis == "x":
                    ref = tok.at[at_x, :, span]
                else:
                    ref = tok.at[:, at_y, span]
                send((r, number, forward, h, i), ref, near(axis, d), s_send.at[r, k], s_recv.at[r, k])

    def landed_stage(r, number):
        for h in (0, 1):
            for i in (0, 1):
                copies[r, number, 1, h, i].wait_recv()

    def weights(s):
        for i, d in enumerate((1, 7)):
            owner = (z - d * s) % 8 * 2 + core
            for part in (0, 1):
                if s > 0:
                    if s == 4 and part != i:
                        continue
                    copies["w", s - 1, i, part].wait_recv()
                ref = w.at[:, pl.ds(owner * 256 + part * 128, 128)]
                if s < 3 or (s == 3 and part == i):
                    to = {"ctx": (z + d) % 8 * 2 + core}
                    send(("w", s, i, part), ref, to, w_send_sem.at[s, i, part], w_recv_sem.at[s, i, part])
                if s > 0 or i == 0:
                    send(
                        ("s", s, i, part), ref, {"ctx": sibling},
                        w_send_sem.at[s, 2 + i, part], w_recv_sem.at[s, 2 + i, part],
                    )

    def tables(t):
        ids = lax.broadcasted_iota(jnp.int32, (8, 128), 0)
        lanes8 = ids.astype(F32)
        cols = pl.ds(t * 128, 128)
        for g in range(3):
            for k in range(3):
                tapb[t, g * 3 + k] = jnp.broadcast_to(taps[g, k : k + 1, cols], (8, 128))
        skipb[t] = jnp.broadcast_to(skip[:, cols], (8, 128))
        for m in range(L):
            filt[t, m] = jnp.zeros((8, 128), F32)
        for n in range(poles):
            lam[t, n] = jnp.broadcast_to(decay[n : n + 1, cols], (8, 128))
            lead[t, n] = jnp.broadcast_to(residues[n : n + 1, cols], (8, 128))

        def mode(n, _):
            rate, gain = lam[t, n], lead[t, n]
            step = jnp.exp(-rate)
            lam[t, n] = step
            lead[t, n] = gain * step
            for k, s in enumerate((1, 2, 4)):
                scan[t, k, n] = jnp.where(ids >= s, jnp.exp(-rate * float(L * s)), 0.0)
            bdec[t, n] = jnp.exp(-rate * (lanes8 * float(L)))
            gdec[t, n] = jnp.exp(-rate * float(GROUP))
            carry[t, n] = jnp.zeros((8, 128), F32)
            for m in range(L):
                filt[t, m] += gain * jnp.exp(-rate * float(m))
            return 0

        lax.fori_loop(0, poles, mode, 0)

    def project(first, size, parts):
        span = pl.ds(first, size)
        left = jnp.concatenate([tok[i // 4, i % 4, span, :] for i in range(16)], axis=1)
        for g in parts:
            total = jnp.dot(left, w[g], preferred_element_type=F32)
            keep(first, size, g, total)

    def keep(first, size, part, total):
        total = total.astype(BF16).astype(F32)
        for t in (0, 1):
            proj[part * 2 + t, pl.ds(HALO + first, size), :] = total[:, t * 128 : (t + 1) * 128]

    def product(first, size, h, part, steps):
        total = None
        for k in steps:
            for i in range(4):
                at_x, at_y = (i, (y + k) % 4) if h == 0 else ((x + k) % 4, i)
                rows_of = pl.ds(pl.multiple_of((at_x * 4 + at_y) * 256, 256), 256)
                one = jnp.dot(
                    tok[at_x, at_y, pl.ds(first, size), :], w[part, rows_of, :], preferred_element_type=F32
                )
                total = one if total is None else total + one
        return total

    def begin(r):
        for _, _, first, size, h in halves(r):
            for part in range(3):
                partial[part, pl.ds(first - LATE, size), :] = product(first, size, h, part, (0, 1, 3))

    def complete(r, parts):
        for _, _, first, size, h in halves(r):
            for part in parts:
                total = partial[part, pl.ds(first - LATE, size), :] + product(first, size, h, part, (2,))
                keep(first, size, part, total)

    def features(g, t, part):
        first = HALO + g * GROUP
        k0, k1, k2 = (tapb[t, part * 3 + k] for k in range(3))
        rows_at = [proj[part * 2 + t, pl.ds(first + i, 8, stride=L), :] for i in range(-2, L)]
        return [k0 * rows_at[i + 2] + k1 * rows_at[i + 1] + k2 * rows_at[i] for i in range(L)]

    def filter_group(g, t, convolve):
        ids = lax.broadcasted_iota(jnp.int32, (8, 128), 0)
        gated = [(a * b).astype(BF16).astype(F32) for a, b in zip(features(g, t, 1), features(g, t, 2))]

        for lo in range(0, poles, 8):
            modes = range(lo, lo + 8)
            steps = [lam[t, n] for n in modes]
            held = [carry[t, n] for n in modes]
            ends = [gated[0]] * 8
            for i in range(1, L):
                ends = [a * b + gated[i] for a, b in zip(steps, ends)]
            for k, s in enumerate((1, 2, 4)):
                ends = [e + scan[t, k, n] * pltpu.roll(e, s, axis=0) for n, e in zip(modes, ends)]
            before = [jnp.where(ids >= 1, pltpu.roll(e, 1, axis=0), 0.0) for e in ends]
            for n, a, b in zip(modes, before, held):
                states[g, t, n] = a + bdec[t, n] * b
            for n, e, b in zip(modes, ends, held):
                carry[t, n] = jnp.broadcast_to(e[7:8], (8, 128)) + gdec[t, n] * b
        if convolve:
            convolve_group(g, t, gated)
        else:
            for i in range(L):
                base[g, t, i] = gated[i]

    def convolve_group(g, t, gated):
        for i, value in enumerate(features(g, t, 0)):
            query[g, t, i] = value
        taken = [filt[t, m] for m in range(L)]
        totals = [skipb[t] * a for a in gated]
        for j in range(L):
            for i in range(j, L):
                totals[i] = totals[i] + taken[i - j] * gated[j]
        for i in range(L):
            base[g, t, i] = totals[i]

    def filter_groups(lo, hi, convolve=True):
        def step(k, _):
            filter_group(lo + k // 2, k % 2, convolve)
            return 0

        lax.fori_loop(0, 2 * (hi - lo), step, 0)

    def convolve_groups(lo, hi):
        def step(k, _):
            g, t = lo + k // 2, k % 2
            convolve_group(g, t, [base[g, t, i] for i in range(L)])
            return 0

        lax.fori_loop(0, 2 * (hi - lo), step, 0)

    def finish(g, _):
        span = pl.ds(pl.multiple_of(g * GROUP, GROUP), GROUP)
        for t in (0, 1):
            flow, steps = [], [lam[t, n] for n in range(poles)]
            for n in range(poles):
                held = entry[t, n]
                flow.append(lead[t, n] * (states[g, t, n] + bdec[t, n] * held))
                entry[t, n] = gdec[t, n] * held
            for i in range(L):
                parts = flow
                while len(parts) > 1:
                    parts = [a + b for a, b in zip(parts[::2], parts[1::2])]
                mixed[t, pl.ds(g * GROUP + i, 8, stride=L), :] = query[g, t, i] * (base[g, t, i] + parts[0])
                if i < L - 1:
                    flow = [a * b for a, b in zip(flow, steps)]
            out[span, t * 128 : (t + 1) * 128] = mixed[t, span, :].astype(BF16)
        return 0

    count = len(CHUNKS)
    stage(0, 1, 0)
    weights(0)
    for r in range(1, count):
        stage(r, 1, 0)
    for r in range(count):
        stage(r, 1, 1)
    weights(1)
    landed_stage(0, 1)
    stage(0, 2, 0)
    landed_stage(1, 1)
    stage(1, 2, 0)
    for r in range(2, count):
        landed_stage(r, 1)

    def tick(r):
        stage(r, 2, 1)
        if r + 2 < count:
            stage(r + 2, 2, 0)

    def compute(r, parts=(0, 1, 2)):
        landed_stage(r, 2)
        project(*CHUNKS[r], parts)

    for copy in small:
        copy.wait()
    tables(0)
    tick(0)
    tables(1)
    weights(2)
    tick(1)
    weights(3)
    tick(2)
    weights(4)
    for key, copy in copies.items():
        if key[0] == "s":
            copy.wait_recv()
    compute(0)
    halo = pltpu.make_async_remote_copy(
        src_ref=proj.at[:, pl.ds(rows, HALO)], dst_ref=proj.at[:, pl.ds(0, HALO)],
        send_sem=h_send, recv_sem=h_recv,
        device_id={"ctx": (ctx + 1) % nctx}, device_id_type=MESH,
    )

    @pl.when(ctx == 0)
    def _():
        proj[:, pl.ds(0, HALO), :] = jnp.zeros((6, HALO, 128), F32)

    @pl.when(ctx < nctx - 1)
    def _():
        halo.start()

    compute(1)
    tick(3)

    @pl.when(ctx > 0)
    def _():
        halo.wait_recv()

    filter_groups(0, 5)
    early = len(sent)
    compute(2)
    tick(4)
    filter_groups(5, 8)
    begin(3)
    for copy in sent[:early]:
        copy.wait_send()
    landed_stage(3, 2)
    complete(3, (0, 1, 2))
    filter_groups(8, 10, False)
    compute(4, (1, 2))
    filter_groups(10, 12, False)

    for t in (0, 1):
        final[:, t * 128 : (t + 1) * 128] = jnp.concatenate([carry[t, n, 0:1, :] for n in range(poles)], axis=0).astype(BF16)

    def exchange(o, slot):
        return pltpu.make_async_remote_copy(
            src_ref=final, dst_ref=landed.at[slot],
            send_sem=f_send.at[o], recv_sem=f_recv.at[o],
            device_id={"ctx": (ctx + o) % nctx}, device_id_type=MESH,
        )

    for o in range(1, nctx):

        @pl.when(ctx + o < nctx)
        def _():
            exchange(o, ctx).start()

    project(*CHUNKS[4], (0,))
    convolve_groups(8, 12)
    for copy in sent[early:]:
        copy.wait_send()
    across = jnp.exp(-decay[...] * float(rows))
    for o in range(1, nctx):

        @pl.when(ctx >= o)
        def _():
            exchange(o, (ctx - o) % nctx).wait_recv()

    def join(k, total):
        return across * total + landed[k].astype(F32)

    incoming = lax.fori_loop(0, ctx, join, jnp.zeros((poles, 256), F32))
    for t in (0, 1):
        for n in range(poles):
            entry[t, n] = jnp.broadcast_to(incoming[n : n + 1, t * 128 : (t + 1) * 128], (8, 128))
    lax.fori_loop(0, groups, finish, 0)


    @pl.when(ctx < nctx - 1)
    def _():
        halo.wait_send()

    for o in range(1, nctx):

        @pl.when(ctx + o < nctx)
        def _():
            exchange(o, ctx).wait_send()


def body(tokens, in_weight, short_taps, residues, decay_rates, skip_gain):
    rows, poles = tokens.shape[0], residues.shape[0]
    groups = rows // GROUP
    flops = 2 * rows * 4096 * 768
    dma = pltpu.SemaphoreType.DMA
    anywhere = pl.BlockSpec(memory_space=pl.ANY)
    return pl.pallas_call(
        kernel,
        out_shape=pltpu.VMEM((rows, 256), BF16),
        in_specs=[anywhere] * 6,
        out_specs=pl.BlockSpec(memory_space=pltpu.VMEM),
        scratch_shapes=[
            pltpu.VMEM((3, 3, 256), F32),
            pltpu.VMEM((poles, 256), F32),
            pltpu.VMEM((poles, 256), F32),
            pltpu.VMEM((1, 256), F32),
            pltpu.VMEM((4, 4, rows, 256), BF16),
            pltpu.VMEM((3, 4096, 256), BF16),
            pltpu.VMEM((6, HALO + rows + L, 128), F32),
            pltpu.VMEM((groups, 2, L, 8, 128), F32),
            pltpu.VMEM((groups, 2, L, 8, 128), F32),
            pltpu.VMEM((groups, 2, poles, 8, 128), F32),
            pltpu.VMEM((2, rows + L, 128), F32),
            pltpu.VMEM((2, poles, 8, 128), F32),
            pltpu.VMEM((2, poles, 8, 128), F32),
            pltpu.VMEM((2, L, 8, 128), F32),
            pltpu.VMEM((2, 3, poles, 8, 128), F32),
            pltpu.VMEM((2, poles, 8, 128), F32),
            pltpu.VMEM((2, poles, 8, 128), F32),
            pltpu.VMEM((2, poles, 8, 128), F32),
            pltpu.VMEM((2, 9, 8, 128), F32),
            pltpu.VMEM((2, 8, 128), F32),
            pltpu.VMEM((poles, 256), BF16),
            pltpu.VMEM((16, poles, 256), BF16),
            pltpu.VMEM((2, poles, 8, 128), F32),
            pltpu.VMEM((3, 256, 256), F32),
            dma((len(CHUNKS), 16)),
            dma((len(CHUNKS), 16)),
            dma((5, 4, 2)),
            dma((5, 4, 2)),
            dma(()),
            dma(()),
            dma((16,)),
            dma((16,)),
            dma((6,)),
        ],
        compiler_params=pltpu.CompilerParams(
            collective_id=0, has_side_effects=True, vmem_limit_bytes=56 * 2**20
        ),
        cost_estimate=pl.CostEstimate(flops=flops, bytes_accessed=4 * 2**20, transcendentals=0),
    )(tokens, in_weight.transpose(1, 0, 2), short_taps, residues, decay_rates, skip_gain.reshape(1, 256))


def solution(mesh):
    in_specs = (
        P("ctx", "ch"),
        P("ctx", None, "ch"),
        P(None, None, "ch"),
        P(None, "ch"),
        P(None, "ch"),
        P("ch"),
    )
    return jax.shard_map(body, mesh=mesh, in_specs=in_specs, out_specs=P("ctx", "ch"), check_vma=False)
```
